512 devices in a mesh: tm: 64 (over x, y, core), space: 8 (over z).
Axes of the slice: x: 4, y: 8, z: 8, core: 2. Of those that a mesh axis runs over, the one named last changes fastest.
Arguments:
- x_in: bfloat16 [128, 1024, 1024], P('tm', 'space'), may hold values from -6 to 6
- b_in: bfloat16 [128, 1024, 128], P('tm', 'space'), may hold values from -0.625 to 0.625
- c_in: bfloat16 [128, 1024, 128], P('tm', 'space'), may hold values from -0.625 to 0.625
- decay_log: float32 [128, 1024, 16], P('tm', 'space'), as said below
- qkv: bfloat16 [128, 1024, 3072], P('tm', 'space'), as said below
- block_of: int32 [128, 1024], P('tm', 'space'), may hold values from 0 to 31, as said below
- norm_gain: float32 [1024], replicated, may hold values from 0.1 to 1.9
Outputs:
- mixed: bfloat16 [128, 1024, 1024], P('tm', 'space')
The draws below stay inside these ranges and needn't reach their ends.
Inputs may be any that keep to these rules, and one draw needn't show every extreme that they name: `block_of`: blocks o*4 to (o+1)*4 - 1 belong to space index o. Of one frame's tile of 128 tokens at most 32 lie in the blocks of one space index, and in every frame some space index holds exactly 32 tokens from every tile. `decay_log`: log decays, never positive. `qkv`: queries, keys and values, each 16 heads of 64 features.
All inputs are finite; a program needn't handle non-finite values.
Results may differ from the reference program's by a relative error of at most 0.005.
Values may be sent and summed in bfloat16 or wider, within the bound.
A program may use at most 128 MiB of HBM per device.

```python
import jax
import jax.numpy as jnp
from jax import lax

D = 1024
H = 16
P_SIZE = 64
N = 128
PATCH_POINTS = 128
BLK_DEV = 4
F_DEV = 2
HORIZON_IMAGES = 128
IMAGE_POINTS = 1024
CAP = 32
N_TM = 64
N_SPACE = 8


def draw_block_of(key, part):
    key = jax.random.fold_in(key, 11)
    busy_key, order_key, local_key = jax.random.split(key, 3)
    busy = jax.random.randint(busy_key, (HORIZON_IMAGES, 1, 1), 0, N_SPACE)
    positions = jnp.arange(PATCH_POINTS, dtype=jnp.int32)[None, None, :]
    others = max(N_SPACE - 1, 1)
    pattern = jnp.where(positions < CAP, busy, (busy + 1 + (positions - CAP) % others) % N_SPACE)
    pattern = jnp.broadcast_to(pattern, (HORIZON_IMAGES, N_SPACE, PATCH_POINTS))
    order_keys = jax.random.split(order_key, HORIZON_IMAGES * N_SPACE)
    orders = jax.vmap(lambda item: jax.random.permutation(item, PATCH_POINTS))(order_keys).reshape(HORIZON_IMAGES, N_SPACE, PATCH_POINTS)
    owners = jnp.take_along_axis(pattern, orders, axis=2)
    within = jax.random.randint(local_key, (HORIZON_IMAGES, N_SPACE, PATCH_POINTS), 0, BLK_DEV)
    return (owners * BLK_DEV + within).reshape(HORIZON_IMAGES, IMAGE_POINTS).astype(jnp.int32)


def log_spread(head_pick, low_end, high_end):
    return jnp.exp(jnp.log(low_end) + head_pick * (jnp.log(high_end) - jnp.log(low_end)))


def draw_decay_log(key, part):
    key = jax.random.fold_in(key, 5)
    stochastic_seeds = jax.random.split(key, 7)
    lasting_count = H // 2
    moderate_count = H // 4
    medium_count = max(H // 8, 1)
    lasting_low = 0.6
    lasting_high = 1.3
    head_order = jax.random.permutation(stochastic_seeds[0], H)
    head_pick = jax.random.uniform(stochastic_seeds[1], (H,))
    chain_len = HORIZON_IMAGES * PATCH_POINTS
    block_len = F_DEV * PATCH_POINTS
    lasting_rate = log_spread(head_pick, lasting_low, lasting_high) / chain_len
    moderate_rate = log_spread(head_pick, 0.06, 0.12) / block_len
    medium_rate = log_spread(head_pick, 1.4, 2.2) / block_len
    fast_rate = log_spread(head_pick, 7.0, 9.0) / block_len
    first_cut = lasting_count
    second_cut = lasting_count + moderate_count
    third_cut = lasting_count + moderate_count + medium_count
    fading_speed = jnp.where(head_order < first_cut, lasting_rate, jnp.where(head_order < second_cut, moderate_rate, jnp.where(head_order < third_cut, medium_rate, fast_rate)))
    image_factor = jnp.exp(jax.random.uniform(stochastic_seeds[3], (HORIZON_IMAGES, 1, 1), minval=-0.7, maxval=0.7))
    small_perturbation = jax.random.uniform(stochastic_seeds[4], (HORIZON_IMAGES, IMAGE_POINTS, H), minval=0.5, maxval=1.5)
    spike_perturbation = jax.random.uniform(stochastic_seeds[5], (HORIZON_IMAGES, IMAGE_POINTS, 1)) < 2.0 / (HORIZON_IMAGES * PATCH_POINTS)
    discarded_elements = jax.random.uniform(stochastic_seeds[6], (HORIZON_IMAGES, IMAGE_POINTS, 1), minval=jnp.log(1.25), maxval=jnp.log(2.0))
    blending_result = -(fading_speed * image_factor * small_perturbation) - jnp.where(spike_perturbation, discarded_elements, 0.0)
    return blending_result.astype(jnp.float32)


def draw_qkv(key, part):
    key = jax.random.fold_in(key, 7)
    stochastic_seeds = jax.random.split(key, 1)
    base = jax.random.normal(stochastic_seeds[0], (HORIZON_IMAGES, IMAGE_POINTS, 3, H, P_SIZE), jnp.float32)
    return base.reshape(HORIZON_IMAGES, IMAGE_POINTS, 3 * D).astype(jnp.bfloat16)


def block_levels(rng, dims, cuts, low, high):
    loudness = 1.0
    for axis_at, shards_of in cuts:
        draws = jax.random.uniform(jax.random.fold_in(jax.random.fold_in(rng, 6), axis_at), (shards_of,), jnp.float32, low / len(cuts), high / len(cuts))
        loudness = loudness * jnp.repeat(jnp.exp(draws), dims[axis_at] // shards_of).reshape((-1,) + (1,) * (len(dims) - 1 - axis_at))
    return loudness


def bell_draw(key, dims, scale, most, cuts=(), held_as=jnp.bfloat16):
    values = jax.random.normal(key, dims, jnp.float32) * scale
    if len(cuts) > 0:
        values = block_levels(key, dims, cuts, -0.22, 0.18) * values
    return jnp.clip(values, min=-most, max=most).astype(held_as)


def setup_inputs(seed: int = 0) -> dict:
    key_list = jax.random.split(jax.random.key(seed), 8)
    x_in = bell_draw(key_list[0], (HORIZON_IMAGES, IMAGE_POINTS, D), 1.0, 6.0, ((0, 64), (1, 8)))
    b_in = bell_draw(key_list[1], (HORIZON_IMAGES, IMAGE_POINTS, N), 0.1, 0.625, ((0, 64), (1, 8)))
    c_in = bell_draw(key_list[2], (HORIZON_IMAGES, IMAGE_POINTS, N), 0.1, 0.625, ((0, 64), (1, 8)))
    decay_log = draw_decay_log(jax.random.fold_in(key_list[7], 71), 0)
    qkv = draw_qkv(jax.random.fold_in(key_list[7], 71), 0)
    block_of = draw_block_of(jax.random.fold_in(key_list[7], 71), 0)
    norm_gain = jnp.clip(1.0 + 0.18 * jax.random.normal(key_list[6], (D,), jnp.float32), 0.1, 1.9)
    return {"x_in": x_in, "b_in": b_in, "c_in": c_in, "decay_log": decay_log, "qkv": qkv, "block_of": block_of, "norm_gain": norm_gain}


def block_scan(carried, pieces):
    inputs_x, inputs_b, inputs_c, log_decay = pieces
    seq_len = log_decay.shape[0]
    running = jnp.cumsum(log_decay, axis=0)
    running_t = running.T
    spread = running_t[:, :, None] - running_t[:, None, :]
    rows_at = lax.broadcasted_iota(jnp.int32, (seq_len, seq_len), 0)
    cols_at = lax.broadcasted_iota(jnp.int32, (seq_len, seq_len), 1)
    lower = (cols_at <= rows_at)[None]
    decay_mat = jnp.where(lower, jnp.exp(jnp.minimum(spread, 0.0)), 0.0)
    gram = jnp.dot(inputs_c, inputs_b.T, preferred_element_type=jnp.float32)
    mixing = (gram[None] * decay_mat).astype(jnp.bfloat16)
    inside = jnp.einsum('hts,shp->thp', mixing.astype(jnp.float32), inputs_x.astype(jnp.float32))
    from_carry = jnp.exp(running)[:, :, None] * jnp.einsum('tn,hpn->thp', inputs_c.astype(jnp.float32), carried, precision=lax.Precision.HIGHEST)
    tail = jnp.exp(running[-1][None, :] - running)
    weighted = (inputs_x.astype(jnp.float32) * tail[:, :, None]).astype(jnp.bfloat16)
    local_state = jnp.einsum('shp,sn->hpn', weighted.astype(jnp.float32), inputs_b.astype(jnp.float32))
    updated = jnp.exp(running[-1])[:, None, None] * carried + local_state
    return (updated, inside + from_carry)

def attend(query, stochastic_seeds, values, query_labels, key_labels):
    scale = query.shape[-1] ** (-0.5)
    scores = jnp.einsum('thp,uhp->htu', query.astype(jnp.float32), stochastic_seeds.astype(jnp.float32)) * scale
    same = (query_labels[:, None] == key_labels[None, :])[None]
    masked = jnp.where(same, scores, -1e+30)
    highest = lax.optimization_barrier(jnp.max(masked, axis=-1, keepdims=True))
    weights = jnp.where(same, jnp.exp(masked - highest), 0.0)
    probs = (weights / lax.optimization_barrier(jnp.sum(weights, axis=-1, keepdims=True))).astype(jnp.bfloat16)
    attended = jnp.einsum('htu,uhp->thp', probs.astype(jnp.float32), values.astype(jnp.float32))
    return attended.reshape(query.shape[0], -1).astype(jnp.bfloat16)

def frame_attention(pieces):
    rows, labels = pieces
    split = rows.reshape(IMAGE_POINTS, 3, H, P_SIZE)
    return attend(split[:, 0], split[:, 1], split[:, 2], labels, labels)

def to_tiles(array):
    tail_shape = array.shape[2:]
    shaped = array.reshape((N_TM, F_DEV, N_SPACE, PATCH_POINTS) + tail_shape)
    shaped = jnp.moveaxis(shaped, 2, 0)
    return shaped.reshape((N_SPACE, N_TM, F_DEV * PATCH_POINTS) + tail_shape)

def reference(x_in, b_in, c_in, decay_log, qkv, block_of, norm_gain):
    x_tiles = to_tiles(x_in.reshape(HORIZON_IMAGES, IMAGE_POINTS, H, P_SIZE))
    b_tiles = to_tiles(b_in)
    c_tiles = to_tiles(c_in)
    d_tiles = to_tiles(decay_log)

    def one_tile(pieces):
        start = jnp.zeros((H, P_SIZE, N), jnp.float32)
        final, outputs = lax.scan(block_scan, start, pieces)
        return outputs
    scanned = lax.map(one_tile, (x_tiles, b_tiles, c_tiles, d_tiles))
    scanned = scanned.reshape(N_SPACE, N_TM, F_DEV, PATCH_POINTS, H, P_SIZE)
    scanned = jnp.moveaxis(scanned, 0, 2).reshape(HORIZON_IMAGES, IMAGE_POINTS, H, P_SIZE)
    mean_sq = lax.optimization_barrier(jnp.mean(scanned * scanned, axis=-1, keepdims=True))
    normed = (scanned * lax.rsqrt(mean_sq + 1e-05)).reshape(HORIZON_IMAGES, IMAGE_POINTS, D) * norm_gain
    attended = lax.map(frame_attention, (qkv, block_of))
    return (normed + attended.astype(jnp.float32)).astype(jnp.bfloat16)
```

```python
import functools
import math

import jax
import jax.numpy as jnp
from jax import lax
from jax.experimental import pallas as pl
from jax.experimental.pallas import tpu as pltpu
from jax.sharding import PartitionSpec as P

MESH = pl.DeviceIdType.MESH
F32 = jnp.float32
BF16 = jnp.bfloat16
HIGHEST = lax.Precision.HIGHEST

FRAMES = 2
TILE = 128
LANES = 128
ROWS = FRAMES * TILE
STATE = 128
UNIT = STATE // 2
PAD = UNIT + 8


def mixer_kernel(
    pairs, row_len, col_len,
    x_hbm, b_hbm, c_hbm, decay_hbm, qkv_hbm, label_hbm, gain_hbm, out_ref,
    x_ref, b_ref, c_ref, decay_ref, gain_ref, load_sem, qkv_ref, qkv_out, qkv_in, v_ones, label_rows, labels, att, att_out, run_col, run_row, gram, inside, normed,
    state_out, state_in, before, before_decay, total_in, enter_out, entering,
    qkv_send, qkv_recv, label_send, label_recv, state_send, state_recv,
    total_send, total_recv, enter_send, enter_recv, att_send, att_recv,
):
    n_space = pairs
    tm = lax.axis_index("tm")
    z = lax.axis_index("space")
    col = lax.div(tm, row_len)
    j = lax.rem(tm, row_len)
    lane = lax.broadcasted_iota(jnp.int32, (1, LANES), 1)
    first_head = lane < LANES // 2

    def space_peer(d):
        return (tm, lax.rem(z + d, n_space))

    def row_peer(d):
        return (col * row_len + lax.rem(j + d, row_len), z)

    def col_peer(d):
        return (lax.rem(col + d, col_len) * row_len + j, z)

    loads = [
        pltpu.make_async_copy(src, dst, load_sem.at[k])
        for k, (src, dst) in enumerate(
            (
                (qkv_hbm.at[pl.ds(0, TILE)], qkv_ref.at[0]),
                (qkv_hbm.at[pl.ds(TILE, TILE)], qkv_ref.at[1]),
                (label_hbm, labels.at[z]),
                (decay_hbm, decay_ref),
                (x_hbm, x_ref),
                (b_hbm, b_ref),
                (c_hbm, c_ref),
                (gain_hbm, gain_ref),
            )
        )
    ]
    for load in loads:
        load.start()

    barrier = pltpu.get_barrier_semaphore()
    for d in range(1, n_space):
        pl.semaphore_signal(barrier, inc=1, device_id=space_peer(d), device_id_type=MESH)
    for d in range(1, row_len):
        pl.semaphore_signal(barrier, inc=1, device_id=row_peer(d), device_id_type=MESH)
    for d in range(1, col_len):
        pl.semaphore_signal(barrier, inc=1, device_id=col_peer(d), device_id_type=MESH)

    def pack(f):
        loads[f].wait()
        for k in range(3 * n_space):
            qkv_out[f, k] = qkv_ref[f, :, k * LANES : (k + 1) * LANES]
        for part in range(3):
            qkv_in[f, part, z] = qkv_out[f, part * n_space + z]

    pack(0)
    pl.semaphore_wait(barrier, n_space + row_len + col_len - 3)

    def qkv_copy(f, part, d, slot):
        dest = lax.rem(z + d, n_space)
        return pltpu.make_async_remote_copy(
            src_ref=qkv_out.at[f, part * n_space + dest],
            dst_ref=qkv_in.at[f, part, slot],
            send_sem=qkv_send.at[f, part, d],
            recv_sem=qkv_recv.at[f, part, d],
            device_id=space_peer(d),
            device_id_type=MESH,
        )

    def label_copy(d, slot):
        return pltpu.make_async_remote_copy(
            src_ref=label_hbm,
            dst_ref=labels.at[slot],
            send_sem=label_send.at[d],
            recv_sem=label_recv.at[d],
            device_id=space_peer(d),
            device_id_type=MESH,
        )

    order = sorted(range(1, n_space), key=lambda d: -min(d, n_space - d))
    for d in order:
        label_copy(d, z).start()

    def send_qkv(f):
        for part in (1, 2, 0):
            for d in order:
                qkv_copy(f, part, jnp.where(lax.rem(tm, 2) == 0, d, n_space - d), z).start()

    send_qkv(0)
    for load in loads[FRAMES:]:
        load.wait()

    rows_at = lax.broadcasted_iota(jnp.int32, (ROWS, ROWS), 0)
    cols_at = lax.broadcasted_iota(jnp.int32, (ROWS, ROWS), 1)
    tri = jnp.where(cols_at <= rows_at, 1.0, 0.0).astype(F32)
    decay_t = jnp.concatenate([decay_ref[f] for f in range(FRAMES)], axis=1)
    running_t = lax.dot_general(
        decay_t, tri, (((1,), (1,)), ((), ())), precision=HIGHEST, preferred_element_type=F32
    )
    running = jnp.concatenate(
        [running_t, jnp.zeros((LANES - 2 * pairs, ROWS), F32)], axis=0
    ).T
    for h in range(2 * pairs):
        run_col[h] = jnp.broadcast_to(running[:, h : h + 1], (ROWS, LANES))
        run_row[h] = running_t[h : h + 1, :]
    b_t = b_ref[...].astype(F32).T.astype(BF16)

    def state_pair(g, _):
        lanes = pl.ds(pl.multiple_of(g * LANES, LANES), LANES)
        merged = jnp.where(first_head, run_col[2 * g], run_col[2 * g + 1])
        last = merged[ROWS - 1 : ROWS, :]
        weighted = (x_ref[:, lanes].astype(F32) * jnp.exp(last - merged)).astype(BF16)
        local_state = jnp.dot(b_t, weighted, preferred_element_type=F32)
        block_decay = jnp.broadcast_to(jnp.exp(last), (PAD - UNIT, LANES))
        for k in range(2):
            state_out[2 * g + k, 0:UNIT, :] = local_state[k * UNIT : (k + 1) * UNIT]
            state_out[2 * g + k, UNIT:PAD, :] = block_decay
        return 0

    def scan_pair(g, _):
        lanes = pl.ds(pl.multiple_of(g * LANES, LANES), LANES)
        x_pair = x_ref[:, lanes]
        parts = []
        lower = cols_at <= rows_at
        for k in range(2):
            at_t = run_col[2 * g + k]
            spread = jnp.concatenate([at_t] * (ROWS // LANES), axis=1) - run_row[2 * g + k]
            mixing = (gram[...] * jnp.exp(jnp.where(lower, spread, -jnp.inf))).astype(BF16)
            parts.append(jnp.dot(mixing, x_pair, preferred_element_type=F32))
        inside[g] = jnp.where(first_head, parts[0], parts[1])
        return 0

    def state_copy(d, slot):
        return pltpu.make_async_remote_copy(
            src_ref=state_out.at[lax.rem(j + d, row_len)],
            dst_ref=state_in.at[slot],
            send_sem=state_send.at[d],
            recv_sem=state_recv.at[d],
            device_id=row_peer(d),
            device_id_type=MESH,
        )

    def total_copy(d, slot):
        return pltpu.make_async_remote_copy(
            src_ref=total_in.at[col],
            dst_ref=total_in.at[slot],
            send_sem=total_send.at[d],
            recv_sem=total_recv.at[d],
            device_id=col_peer(d),
            device_id_type=MESH,
        )

    def enter_copy(d, slot):
        return pltpu.make_async_remote_copy(
            src_ref=enter_out.at[lax.rem(j + d, row_len)],
            dst_ref=entering.at[slot],
            send_sem=enter_send.at[d],
            recv_sem=enter_recv.at[d],
            device_id=row_peer(d),
            device_id_type=MESH,
        )

    lax.fori_loop(0, pairs, state_pair, 0)
    for d in range(1, row_len):
        state_copy(d, j).start()
    state_in[j] = state_out[j]
    gram[...] = lax.dot_general(
        c_ref[...], b_ref[...], (((1,), (1,)), ((), ())), preferred_element_type=F32
    )
    lax.fori_loop(0, pairs, scan_pair, 0)
    pack(1)
    send_qkv(1)

    def row_prefix():
        for d in range(1, row_len):
            state_copy(d, lax.rem(j - d + row_len, row_len)).wait_recv()

        def step(i, carried):
            state, through = carried
            before[i] = state
            before_decay[i] = through
            here = state_in[i, UNIT:PAD, :]
            return here[0:1] * state + state_in[i, 0:UNIT, :], here * through

        state, through = lax.fori_loop(
            0, row_len, step, (jnp.zeros((UNIT, LANES), F32), jnp.ones((PAD - UNIT, LANES), F32))
        )
        total_in[col, 0:UNIT, :] = state
        total_in[col, UNIT:PAD, :] = through
        for d in range(1, col_len):
            total_copy(d, col).start()

    def col_prefix():
        for d in range(1, col_len):
            total_copy(d, lax.rem(col - d + col_len, col_len)).wait_recv()
        carry = jnp.zeros((UNIT, LANES), F32)
        for i in range(col_len - 1):
            new = total_in[i, UNIT : UNIT + 1, :] * carry + total_in[i, 0:UNIT, :]
            carry = jnp.where(i < col, new, carry)

        def step(i, _):
            enter_out[i] = before[i] + before_decay[i, 0:1, :] * carry
            return 0

        lax.fori_loop(0, row_len, step, 0)
        for d in range(1, row_len):
            enter_copy(d, j).start()
        entering[j] = enter_out[j]

    def finish_scan():
        for d in range(1, row_len):
            enter_copy(d, lax.rem(j - d + row_len, row_len)).wait_recv()
        rows_half = lax.broadcasted_iota(jnp.int32, (LANES, LANES), 0) < LANES // 2
        cols_half = lax.broadcasted_iota(jnp.int32, (LANES, LANES), 1) < LANES // 2
        averager = jnp.where(rows_half == cols_half, 2.0 / LANES, 0.0).astype(F32)

        def norm_pair(g, _):
            state = jnp.concatenate([entering[2 * g], entering[2 * g + 1]], axis=0)
            high = state.astype(BF16)
            low = (state - high.astype(F32)).astype(BF16)
            c_in = c_ref[...]
            carried = jnp.dot(c_in, high, preferred_element_type=F32) + jnp.dot(
                c_in, low, preferred_element_type=F32
            )
            merged = jnp.where(first_head, run_col[2 * g], run_col[2 * g + 1])
            scanned = inside[g] + jnp.exp(merged) * carried
            mean_sq = jnp.dot(
                scanned * scanned, averager, precision=HIGHEST, preferred_element_type=F32
            )
            lanes = pl.ds(pl.multiple_of(g * LANES, LANES), LANES)
            normed[g] = scanned * lax.rsqrt(mean_sq + 1e-05) * gain_ref[:, lanes]
            return 0

        lax.fori_loop(0, pairs, norm_pair, 0)

    def att_copy(f, d, tile, slot):
        return pltpu.make_async_remote_copy(
            src_ref=att_out.at[f, tile],
            dst_ref=att.at[f, slot],
            send_sem=att_send.at[f, d],
            recv_sem=att_recv.at[f, d],
            device_id=space_peer(d),
            device_id_type=MESH,
        )

    def wait_qkv(f, part):
        for d in order:
            qkv_copy(f, part, d, lax.rem(z - d + n_space, n_space)).wait_recv()

    rate = (LANES // 2) ** (-0.5) * math.log2(math.e)
    eye = lax.broadcasted_iota(jnp.int32, (TILE, TILE), 0) == lax.broadcasted_iota(
        jnp.int32, (TILE, TILE), 1
    )

    def attend(f):
        v_ones[:, 0:LANES] = qkv_in[f, 2].reshape(n_space * TILE, LANES)
        label_row = jnp.concatenate(
            [labels[s, f : f + 1, :] for s in range(n_space)], axis=1
        )
        label_rows[...] = label_row.astype(F32)
        keep = [
            jnp.where(first_head, 1.0, 0.0).astype(BF16),
            jnp.where(first_head, 0.0, 1.0).astype(BF16),
        ]

        def step(i, _):
            offsets = (n_space // 2 - i, n_space // 2 + 1 + i)
            tiles = [lax.rem(z + d, n_space) for d in offsets]
            last = i == n_space // 2 - 1

            qkv_copy(f, 0, n_space - offsets[0], tiles[0]).wait_recv()

            @pl.when(jnp.logical_not(last))
            def _():
                qkv_copy(f, 0, n_space - offsets[1], tiles[1]).wait_recv()

            query = [qkv_in[f, 0, tile] for tile in tiles]
            rows = jnp.concatenate([q * k for q in query for k in keep], axis=0)
            keys = qkv_in[f, 1].reshape(n_space * TILE, LANES)
            scores = lax.dot_general(
                rows, keys, (((1,), (1,)), ((), ())), preferred_element_type=F32
            ).reshape(2, 2, TILE, n_space * TILE)
            same = []
            for tile in tiles:
                own_row = labels[tile, f : f + 1, :].astype(F32)
                own_col = jnp.sum(jnp.where(eye, own_row, 0.0), axis=1, keepdims=True)
                same.append((own_col == label_rows[...])[None, None])
            weights = []
            for k in range(2):
                masked = jnp.where(same[k][0], scores[k], -jnp.inf)
                highest = jnp.max(masked, axis=-1, keepdims=True)
                weights.append(jnp.exp2((masked - highest) * rate).astype(BF16))
            summed = jnp.dot(
                jnp.concatenate(weights, axis=0).reshape(4 * TILE, n_space * TILE),
                v_ones[...],
                preferred_element_type=F32,
            ).reshape(2, 2, TILE, 2 * LANES)
            merged = jnp.where(first_head, summed[:, 0, :, 0:LANES], summed[:, 1, :, 0:LANES])
            total = jnp.where(first_head, summed[:, 0, :, LANES:], summed[:, 1, :, LANES:])
            result = (merged / total).astype(BF16)
            for k in range(2):
                att_out[f, tiles[k]] = result[k]
            att_copy(f, offsets[0], tiles[0], z).start()

            @pl.when(jnp.logical_not(last))
            def _():
                att_copy(f, offsets[1], tiles[1], z).start()

            return 0

        lax.fori_loop(0, n_space // 2, step, 0)
        att[f, z] = att_out[f, z]

    v_ones[:, LANES : 2 * LANES] = jnp.ones((n_space * TILE, LANES), BF16)
    row_prefix()
    for d in order:
        label_copy(d, lax.rem(z - d + n_space, n_space)).wait_recv()
    for f in range(FRAMES):
        wait_qkv(f, 1)
        wait_qkv(f, 2)
        attend(f)
        if f == 0:
            col_prefix()
    finish_scan()

    for d in order:
        label_copy(d, z).wait_send()
        for f in range(FRAMES):
            for part in range(3):
                qkv_copy(f, part, d, z).wait_send()
    for d in range(1, row_len):
        state_copy(d, j).wait_send()
        enter_copy(d, j).wait_send()
    for d in range(1, col_len):
        total_copy(d, col).wait_send()

    for f in range(FRAMES):
        for d in range(1, n_space):
            att_copy(f, d, lax.rem(z + d, n_space), lax.rem(z - d + n_space, n_space)).wait_recv()

        def add_pair(g, _):
            lanes = pl.ds(pl.multiple_of(g * LANES, LANES), LANES)
            rows = slice(f * TILE, (f + 1) * TILE)
            out_ref[rows, lanes] = (normed[g, rows, :] + att[f, g].astype(F32)).astype(BF16)
            return 0

        lax.fori_loop(0, pairs, add_pair, 0)

    for f in range(FRAMES):
        for d in order:
            att_copy(f, d, lax.rem(z + d, n_space), z).wait_send()


def hand_on_kernel(src, dst, held, in_sems, out_sems):
    pieces = in_sems.shape[0]
    rows = [pl.ds(k * (ROWS // pieces), ROWS // pieces) for k in range(pieces)]
    reads = [
        pltpu.make_async_copy(src.at[at], held.at[at], in_sems.at[k]) for k, at in enumerate(rows)
    ]
    writes = [
        pltpu.make_async_copy(held.at[at], dst.at[at], out_sems.at[k]) for k, at in enumerate(rows)
    ]
    for read in reads:
        read.start()
    for read, write in zip(reads, writes):
        read.wait()
        write.start()
    for write in writes:
        write.wait()


def solution(mesh):
    n_space = mesh.shape["space"]
    row_len = 16
    col_len = mesh.shape["tm"] // row_len

    def shards(x_in, b_in, c_in, decay_log, qkv, block_of, norm_gain):
        width = x_in.shape[2]
        pairs = width // LANES
        vmem = pl.BlockSpec(memory_space=pltpu.VMEM)
        dma = pltpu.SemaphoreType.DMA
        out = pl.pallas_call(
            functools.partial(mixer_kernel, pairs, row_len, col_len),
            out_shape=jax.ShapeDtypeStruct((ROWS, width), BF16),
            in_specs=[pl.BlockSpec(memory_space=pltpu.HBM)] * 7,
            out_specs=vmem,
            scratch_shapes=[
                pltpu.VMEM((ROWS, width), BF16),
                pltpu.VMEM((ROWS, STATE), BF16),
                pltpu.VMEM((ROWS, STATE), BF16),
                pltpu.VMEM((FRAMES, 2 * pairs, TILE), F32),
                pltpu.VMEM((1, width), F32),
                dma((8,)),
                pltpu.VMEM((FRAMES, TILE, 3 * width), BF16),
                pltpu.VMEM((FRAMES, 3 * pairs, TILE, LANES), BF16),
                pltpu.VMEM((FRAMES, 3, n_space, TILE, LANES), BF16),
                pltpu.VMEM((n_space * TILE, 2 * LANES), BF16),
                pltpu.VMEM((1, n_space * TILE), F32),
                pltpu.VMEM((n_space, FRAMES, TILE), jnp.int32),
                pltpu.VMEM((FRAMES, n_space, TILE, LANES), BF16),
                pltpu.VMEM((FRAMES, n_space, TILE, LANES), BF16),
                pltpu.VMEM((2 * pairs, ROWS, LANES), F32),
                pltpu.VMEM((2 * pairs, 1, ROWS), F32),
                pltpu.VMEM((ROWS, ROWS), F32),
                pltpu.VMEM((pairs, ROWS, LANES), F32),
                pltpu.VMEM((pairs, ROWS, LANES), F32),
                pltpu.VMEM((row_len, PAD, LANES), F32),
                pltpu.VMEM((row_len, PAD, LANES), F32),
                pltpu.VMEM((row_len, UNIT, LANES), F32),
                pltpu.VMEM((row_len, PAD - UNIT, LANES), F32),
                pltpu.VMEM((col_len, PAD, LANES), F32),
                pltpu.VMEM((row_len, UNIT, LANES), F32),
                pltpu.VMEM((row_len, UNIT, LANES), F32),
                dma((FRAMES, 3, n_space)),
                dma((FRAMES, 3, n_space)),
                dma((n_space,)),
                dma((n_space,)),
                dma((row_len,)),
                dma((row_len,)),
                dma((col_len,)),
                dma((col_len,)),
                dma((row_len,)),
                dma((row_len,)),
                dma((FRAMES, n_space)),
                dma((FRAMES, n_space)),
            ],
            compiler_params=pltpu.CompilerParams(
                collective_id=0, has_side_effects=True, vmem_limit_bytes=64 * 1024 * 1024
            ),
        )(
            x_in.reshape(ROWS, width),
            b_in.reshape(ROWS, STATE),
            c_in.reshape(ROWS, STATE),
            jnp.swapaxes(decay_log, 1, 2),
            qkv.reshape(ROWS, 3 * width),
            block_of,
            norm_gain.reshape(1, width),
        )
        hbm = pl.BlockSpec(memory_space=pltpu.HBM)
        out = pl.pallas_call(
            hand_on_kernel,
            out_shape=jax.ShapeDtypeStruct((ROWS, width), BF16),
            in_specs=[hbm],
            out_specs=hbm,
            scratch_shapes=[pltpu.VMEM((ROWS, width), BF16), dma((4,)), dma((4,))],
            compiler_params=pltpu.CompilerParams(vmem_limit_bytes=64 * 1024 * 1024),
        )(out)
        return out.reshape(FRAMES, TILE, width)

    spec = P("tm", "space", None)
    return jax.shard_map(
        shards,
        mesh=mesh,
        in_specs=(spec, spec, spec, spec, spec, P("tm", "space"), P()),
        out_specs=spec,
        check_vma=False,
    )
```

```python
import functools
import math

import jax
import jax.numpy as jnp
from jax import lax
from jax.experimental import pallas as pl
from jax.experimental.pallas import tpu as pltpu
from jax.sharding import PartitionSpec as P

MESH = pl.DeviceIdType.MESH
F32 = jnp.float32
BF16 = jnp.bfloat16
HIGHEST = lax.Precision.HIGHEST

FRAMES = 2
TILE = 128
LANES = 128
ROWS = FRAMES * TILE
STATE = 128
UNIT = STATE // 2
CHUNK = 16
PAD = UNIT + 8


def mixer_kernel(
    pairs, row_len, col_len,
    x_hbm, b_hbm, c_hbm, decay_hbm, qkv_ref, label_hbm, gain_hbm, out_hbm,
    x_ref, b_ref, c_ref, decay_ref, gain_ref, load_sem, qkv_in, v_ones, label_rows, label_cols, scores, weights, labels, att, att_out, run_col, run_row, gram, inside, normed,
    state_out, state_in, before, before_decay, total_in, enter_out, entering,
    qkv_send, qkv_recv, label_send, label_recv, state_send, state_recv,
    total_send, total_recv, enter_send, enter_recv, att_send, att_recv, here_sem, column_sem, out_ref, out_sem,
):
    n_space = pairs
    tm = lax.axis_index("tm")
    z = lax.axis_index("space")
    col = lax.div(tm, row_len)
    j = lax.rem(tm, row_len)
    lane = lax.broadcasted_iota(jnp.int32, (1, LANES), 1)
    first_head = lane < LANES // 2

    def space_peer(d):
        return (tm, lax.rem(z + d, n_space))

    def row_peer(d):
        return (col * row_len + lax.rem(j + d, row_len), z)

    def col_peer(d):
        return (lax.rem(col + d, col_len) * row_len + j, z)

    loads = [
        pltpu.make_async_copy(src, dst, load_sem.at[k])
        for k, (src, dst) in enumerate(
            (
                (label_hbm, labels.at[z]),
                (decay_hbm, decay_ref),
                (x_hbm, x_ref),
                (b_hbm, b_ref),
                (c_hbm, c_ref),
                (gain_hbm, gain_ref),
            )
        )
    ]
    for load in loads:
        load.start()

    barrier = pltpu.get_barrier_semaphore()
    leads = z == 0
    for d in range(1, n_space):

        @pl.when(lax.rem(z + d, n_space) != 0)
        def _(d=d):
            pl.semaphore_signal(barrier, inc=1, device_id=space_peer(d), device_id_type=MESH)

    @pl.when(jnp.logical_not(leads))
    def _():
        pl.semaphore_wait(barrier, n_space - 1)
        pl.semaphore_signal(here_sem, inc=1, device_id=(tm, 0), device_id_type=MESH)

    @pl.when(leads)
    def _():
        pl.semaphore_wait(here_sem, n_space - 1)
        for d in range(1, row_len):
            pl.semaphore_signal(barrier, inc=1, device_id=row_peer(d), device_id_type=MESH)
        for d in range(1, col_len):
            pl.semaphore_signal(barrier, inc=1, device_id=col_peer(d), device_id_type=MESH)

    def wait_columns():
        @pl.when(leads)
        def _():
            pl.semaphore_wait(barrier, row_len + col_len - 2)
            for d in range(1, n_space):
                pl.semaphore_signal(
                    column_sem, inc=1, device_id=space_peer(d), device_id_type=MESH
                )

        @pl.when(jnp.logical_not(leads))
        def _():
            pl.semaphore_wait(column_sem, 1)

    def qkv_copy(f, part, d, slot):
        dest = lax.rem(z + d, n_space)
        lanes = pl.ds(pl.multiple_of((part * n_space + dest) * LANES, LANES), LANES)
        return pltpu.make_async_remote_copy(
            src_ref=qkv_ref.at[pl.ds(f * TILE, TILE), lanes],
            dst_ref=qkv_in.at[f, part, slot],
            send_sem=qkv_send.at[f, part, d],
            recv_sem=qkv_recv.at[f, part, d],
            device_id=space_peer(d),
            device_id_type=MESH,
        )

    def qkv_own(f, part):
        lanes = pl.ds(pl.multiple_of((part * n_space + z) * LANES, LANES), LANES)
        return pltpu.make_async_copy(
            qkv_ref.at[pl.ds(f * TILE, TILE), lanes],
            qkv_in.at[f, part, z],
            qkv_recv.at[f, part, 0],
        )

    def label_copy(d, slot):
        return pltpu.make_async_remote_copy(
            src_ref=label_hbm,
            dst_ref=labels.at[slot],
            send_sem=label_send.at[d],
            recv_sem=label_recv.at[d],
            device_id=space_peer(d),
            device_id_type=MESH,
        )

    def each(count, act):
        def body(i, _):
            act(i)
            return 0

        lax.fori_loop(0, count, body, 0)

    def each_offset(act):
        sign = 1 - 2 * lax.rem(tm, 2)
        each(
            n_space - 1,
            lambda i: act(
                n_space // 2 + lax.div(i + 1, 2) * (1 - 2 * lax.rem(i, 2)) * sign
            ),
        )

    def send_qkv(f, part):
        each_offset(lambda d: qkv_copy(f, part, d, z).start())
        qkv_own(f, part).start()

    parts = (1, 2, 0)
    for part in parts:
        send_qkv(0, part)
    each_offset(lambda d: label_copy(d, z).start())
    for load in loads:
        load.wait()

    rows_at = lax.broadcasted_iota(jnp.int32, (ROWS, ROWS), 0)
    cols_at = lax.broadcasted_iota(jnp.int32, (ROWS, ROWS), 1)
    tri = jnp.where(cols_at <= rows_at, 1.0, 0.0).astype(F32)
    decay_t = jnp.concatenate([decay_ref[f] for f in range(FRAMES)], axis=1)
    running_t = lax.dot_general(
        decay_t, tri, (((1,), (1,)), ((), ())), precision=HIGHEST, preferred_element_type=F32
    )
    running = jnp.concatenate(
        [running_t, jnp.zeros((LANES - 2 * pairs, ROWS), F32)], axis=0
    ).T
    for h in range(2 * pairs):
        run_col[h] = jnp.broadcast_to(running[:, h : h + 1], (ROWS, LANES))
        run_row[h] = running_t[h : h + 1, :]
    b_t = b_ref[...].astype(F32).T.astype(BF16)

    low_tile = lax.broadcasted_iota(jnp.int32, (TILE, TILE), 1) <= lax.broadcasted_iota(
        jnp.int32, (TILE, TILE), 0
    )

    def state_pair(g, _):
        lanes = pl.ds(pl.multiple_of(g * LANES, LANES), LANES)
        merged = jnp.where(first_head, run_col[2 * g], run_col[2 * g + 1])
        last = merged[ROWS - 1 : ROWS, :]
        weighted = (x_ref[:, lanes].astype(F32) * jnp.exp(last - merged)).astype(BF16)
        local_state = jnp.dot(b_t, weighted, preferred_element_type=F32)
        block_decay = jnp.broadcast_to(jnp.exp(last), (PAD - UNIT, LANES))
        for k in range(2):
            state_out[2 * g + k, 0:UNIT, :] = local_state[k * UNIT : (k + 1) * UNIT]
            state_out[2 * g + k, UNIT:PAD, :] = block_decay
        return 0

    def scan_pair(g, _):
        lanes = pl.ds(pl.multiple_of(g * LANES, LANES), LANES)
        x_pair = x_ref[:, lanes]
        early, late = slice(0, TILE), slice(TILE, 2 * TILE)
        first, second = [], []
        for k in range(2):
            h = 2 * g + k

            def mix(rows, cols, masked):
                spread = run_col[h, rows, :] - run_row[h, :, cols]
                if masked:
                    spread = jnp.where(low_tile, spread, -jnp.inf)
                return (gram[rows, cols] * jnp.exp(spread)).astype(BF16)

            first.append(mix(early, early, True))
            second.append(
                jnp.concatenate([mix(late, early, False), mix(late, late, True)], axis=1)
            )
        for rows, mixing, values in (
            (early, first, x_pair[early]),
            (late, second, x_pair),
        ):
            both = jnp.dot(
                jnp.concatenate(mixing, axis=0), values, preferred_element_type=F32
            )
            inside[g, rows, :] = jnp.where(first_head, both[early], both[late])
        return 0

    def state_copy(d, slot):
        return pltpu.make_async_remote_copy(
            src_ref=state_out.at[lax.rem(j + d, row_len)],
            dst_ref=state_in.at[slot],
            send_sem=state_send.at[d],
            recv_sem=state_recv.at[d],
            device_id=row_peer(d),
            device_id_type=MESH,
        )

    def total_copy(d, slot):
        return pltpu.make_async_remote_copy(
            src_ref=total_in.at[col],
            dst_ref=total_in.at[slot],
            send_sem=total_send.at[d],
            recv_sem=total_recv.at[d],
            device_id=col_peer(d),
            device_id_type=MESH,
        )

    def enter_copy(d, slot):
        return pltpu.make_async_remote_copy(
            src_ref=enter_out.at[lax.rem(j + d, row_len)],
            dst_ref=entering.at[slot],
            send_sem=enter_send.at[d],
            recv_sem=enter_recv.at[d],
            device_id=row_peer(d),
            device_id_type=MESH,
        )

    lax.fori_loop(0, pairs, state_pair, 0)
    gram[...] = lax.dot_general(
        c_ref[...], b_ref[...], (((1,), (1,)), ((), ())), preferred_element_type=F32
    )
    lax.fori_loop(0, pairs, scan_pair, 0)
    wait_columns()
    each(row_len - 1, lambda i: state_copy(i + 1, j).start())
    state_in[j] = state_out[j]
    for part in parts:
        each_offset(lambda d: qkv_copy(0, part, d, z).wait_send())
        send_qkv(1, part)

    def row_prefix():
        each(
            row_len - 1,
            lambda i: state_copy(i + 1, lax.rem(j - i - 1 + row_len, row_len)).wait_recv(),
        )

        def step(i, carried):
            state, through = carried
            before[i] = state
            before_decay[i] = through
            here = state_in[i, UNIT:PAD, :]
            return here[0:1] * state + state_in[i, 0:UNIT, :], here * through

        state, through = lax.fori_loop(
            0, row_len, step, (jnp.zeros((UNIT, LANES), F32), jnp.ones((PAD - UNIT, LANES), F32))
        )
        total_in[col, 0:UNIT, :] = state
        total_in[col, UNIT:PAD, :] = through
        for d in range(1, col_len):
            total_copy(d, col).start()

    def col_prefix():
        for d in range(1, col_len):
            total_copy(d, lax.rem(col - d + col_len, col_len)).wait_recv()
        carry = jnp.zeros((UNIT, LANES), F32)
        for i in range(col_len - 1):
            new = total_in[i, UNIT : UNIT + 1, :] * carry + total_in[i, 0:UNIT, :]
            carry = jnp.where(i < col, new, carry)

        def step(i, _):
            enter_out[i] = before[i] + before_decay[i, 0:1, :] * carry
            return 0

        lax.fori_loop(0, row_len, step, 0)
        each(row_len - 1, lambda i: enter_copy(i + 1, j).start())
        entering[j] = enter_out[j]

    def finish_scan():
        each(
            row_len - 1,
            lambda i: enter_copy(i + 1, lax.rem(j - i - 1 + row_len, row_len)).wait_recv(),
        )
        rows_half = lax.broadcasted_iota(jnp.int32, (LANES, LANES), 0) < LANES // 2
        cols_half = lax.broadcasted_iota(jnp.int32, (LANES, LANES), 1) < LANES // 2
        averager = jnp.where(rows_half == cols_half, 2.0 / LANES, 0.0).astype(F32)

        def norm_pair(g, _):
            state = jnp.concatenate([entering[2 * g], entering[2 * g + 1]], axis=0)
            high = state.astype(BF16)
            low = (state - high.astype(F32)).astype(BF16)
            c_in = c_ref[...]
            carried = jnp.dot(c_in, high, preferred_element_type=F32) + jnp.dot(
                c_in, low, preferred_element_type=F32
            )
            merged = jnp.where(first_head, run_col[2 * g], run_col[2 * g + 1])
            scanned = inside[g] + jnp.exp(merged) * carried
            mean_sq = jnp.dot(
                scanned * scanned, averager, precision=HIGHEST, preferred_element_type=F32
            )
            lanes = pl.ds(pl.multiple_of(g * LANES, LANES), LANES)
            normed[g] = scanned * lax.rsqrt(mean_sq + 1e-05) * gain_ref[:, lanes]
            return 0

        lax.fori_loop(0, pairs, norm_pair, 0)

    def att_copy(f, d, tile, slot):
        return pltpu.make_async_remote_copy(
            src_ref=att_out.at[f, tile],
            dst_ref=att.at[f, slot],
            send_sem=att_send.at[f, d],
            recv_sem=att_recv.at[f, d],
            device_id=space_peer(d),
            device_id_type=MESH,
        )

    def wait_qkv(f, part):
        each_offset(
            lambda d: qkv_copy(f, part, d, lax.rem(z - d + n_space, n_space)).wait_recv()
        )
        qkv_own(f, part).wait()

    rate = (LANES // 2) ** (-0.5) * math.log2(math.e)
    def attend(f):
        v_ones[:, 0:LANES] = qkv_in[f, 2].reshape(n_space * TILE, LANES)
        for s in range(n_space):
            row = labels[s, f : f + 1, :].astype(F32)
            label_rows[:, s * LANES : (s + 1) * LANES] = jnp.broadcast_to(row, (CHUNK, LANES))
            label_cols[s] = jnp.broadcast_to(row, (TILE, TILE)).T
        keep = [
            jnp.where(first_head, 1.0, 0.0).astype(BF16),
            jnp.where(first_head, 0.0, 1.0).astype(BF16),
        ]

        def step(i, _):
            offsets = (n_space // 2 - i, n_space // 2 + 1 + i)
            tiles = [lax.rem(z + d, n_space) for d in offsets]
            last = i == n_space // 2 - 1

            qkv_copy(f, 0, n_space - offsets[0], tiles[0]).wait_recv()

            @pl.when(jnp.logical_not(last))
            def _():
                qkv_copy(f, 0, n_space - offsets[1], tiles[1]).wait_recv()

            @pl.when(last)
            def _():
                qkv_own(f, 0).wait()

            query = [qkv_in[f, 0, tile] for tile in tiles]
            rows = jnp.concatenate([q * k for q in query for k in keep], axis=0)
            keys = qkv_in[f, 1].reshape(n_space * TILE, LANES)
            scores[...] = lax.dot_general(
                rows, keys, (((1,), (1,)), ((), ())), preferred_element_type=F32
            )
            for k in range(2):
                for c in range(0, TILE, CHUNK):
                    col = label_cols[tiles[k], c : c + CHUNK, :]
                    same = jnp.concatenate([col] * n_space, axis=1) == label_rows[...]
                    for h in range(2):
                        at = slice((2 * k + h) * TILE + c, (2 * k + h) * TILE + c + CHUNK)
                        masked = jnp.where(same, scores[at, :], -jnp.inf)
                        highest = jnp.max(masked, axis=-1, keepdims=True)
                        weights[at, :] = jnp.exp2((masked - highest) * rate).astype(BF16)
            summed = jnp.dot(
                weights[...], v_ones[...], preferred_element_type=F32
            ).reshape(2, 2, TILE, 2 * LANES)
            merged = jnp.where(first_head, summed[:, 0, :, 0:LANES], summed[:, 1, :, 0:LANES])
            total = jnp.where(first_head, summed[:, 0, :, LANES:], summed[:, 1, :, LANES:])
            result = (merged / total).astype(BF16)
            for k in range(2):
                att_out[f, tiles[k]] = result[k]
            att_copy(f, offsets[0], tiles[0], z).start()

            @pl.when(jnp.logical_not(last))
            def _():
                att_copy(f, offsets[1], tiles[1], z).start()

            return 0

        lax.fori_loop(0, n_space // 2, step, 0)
        att[f, z] = att_out[f, z]

    v_ones[:, LANES : 2 * LANES] = jnp.ones((n_space * TILE, LANES), BF16)
    row_prefix()
    each_offset(lambda d: label_copy(d, lax.rem(z - d + n_space, n_space)).wait_recv())
    for f in range(FRAMES):
        wait_qkv(f, 1)
        wait_qkv(f, 2)
        attend(f)
        if f == 0:
            col_prefix()
    finish_scan()

    def out_copy(f):
        rows = pl.ds(f * TILE, TILE)
        return pltpu.make_async_copy(out_ref.at[rows], out_hbm.at[rows], out_sem.at[f])

    def all_sent(d):
        label_copy(d, z).wait_send()
        for part in parts:
            qkv_copy(1, part, d, z).wait_send()

    def states_sent(i):
        state_copy(i + 1, j).wait_send()
        enter_copy(i + 1, j).wait_send()

    each_offset(all_sent)
    each(row_len - 1, states_sent)
    for d in range(1, col_len):
        total_copy(d, col).wait_send()

    for f in range(FRAMES):
        each_offset(
            lambda d: att_copy(
                f, d, lax.rem(z + d, n_space), lax.rem(z - d + n_space, n_space)
            ).wait_recv()
        )

        def add_pair(g, _):
            lanes = pl.ds(pl.multiple_of(g * LANES, LANES), LANES)
            rows = slice(f * TILE, (f + 1) * TILE)
            out_ref[rows, lanes] = (normed[g, rows, :] + att[f, g].astype(F32)).astype(BF16)
            return 0

        lax.fori_loop(0, pairs, add_pair, 0)
        out_copy(f).start()

    for f in range(FRAMES):
        each_offset(lambda d: att_copy(f, d, lax.rem(z + d, n_space), z).wait_send())
        out_copy(f).wait()


def solution(mesh):
    n_space = mesh.shape["space"]
    row_len = 16
    col_len = mesh.shape["tm"] // row_len

    def shards(x_in, b_in, c_in, decay_log, qkv, block_of, norm_gain):
        width = x_in.shape[2]
        pairs = width // LANES
        dma = pltpu.SemaphoreType.DMA
        out = pl.pallas_call(
            functools.partial(mixer_kernel, pairs, row_len, col_len),
            out_shape=jax.ShapeDtypeStruct((ROWS, width), BF16),
            in_specs=[pl.BlockSpec(memory_space=pltpu.HBM)] * 7,
            out_specs=pl.BlockSpec(memory_space=pltpu.HBM),
            scratch_shapes=[
                pltpu.VMEM((ROWS, width), BF16),
                pltpu.VMEM((ROWS, STATE), BF16),
                pltpu.VMEM((ROWS, STATE), BF16),
                pltpu.VMEM((FRAMES, 2 * pairs, TILE), F32),
                pltpu.VMEM((1, width), F32),
                dma((6,)),
                pltpu.VMEM((FRAMES, 3, n_space, TILE, LANES), BF16),
                pltpu.VMEM((n_space * TILE, 2 * LANES), BF16),
                pltpu.VMEM((CHUNK, n_space * TILE), F32),
                pltpu.VMEM((n_space, TILE, TILE), F32),
                pltpu.VMEM((4 * TILE, n_space * TILE), F32),
                pltpu.VMEM((4 * TILE, n_space * TILE), BF16),
                pltpu.VMEM((n_space, FRAMES, TILE), jnp.int32),
                pltpu.VMEM((FRAMES, n_space, TILE, LANES), BF16),
                pltpu.VMEM((FRAMES, n_space, TILE, LANES), BF16),
                pltpu.VMEM((2 * pairs, ROWS, LANES), F32),
                pltpu.VMEM((2 * pairs, 1, ROWS), F32),
                pltpu.VMEM((ROWS, ROWS), F32),
                pltpu.VMEM((pairs, ROWS, LANES), F32),
                pltpu.VMEM((pairs, ROWS, LANES), F32),
                pltpu.VMEM((row_len, PAD, LANES), F32),
                pltpu.VMEM((row_len, PAD, LANES), F32),
                pltpu.VMEM((row_len, UNIT, LANES), F32),
                pltpu.VMEM((row_len, PAD - UNIT, LANES), F32),
                pltpu.VMEM((col_len, PAD, LANES), F32),
                pltpu.VMEM((row_len, UNIT, LANES), F32),
                pltpu.VMEM((row_len, UNIT, LANES), F32),
                dma((FRAMES, 3, n_space)),
                dma((FRAMES, 3, n_space)),
                dma((n_space,)),
                dma((n_space,)),
                dma((row_len,)),
                dma((row_len,)),
                dma((col_len,)),
                dma((col_len,)),
                dma((row_len,)),
                dma((row_len,)),
                dma((FRAMES, n_space)),
                dma((FRAMES, n_space)),
                pltpu.SemaphoreType.REGULAR,
                pltpu.SemaphoreType.REGULAR,
                pltpu.VMEM((ROWS, width), BF16),
                dma((FRAMES,)),
            ],
            compiler_params=pltpu.CompilerParams(
                collective_id=0, has_side_effects=True, vmem_limit_bytes=64 * 1024 * 1024
            ),
        )(
            x_in.reshape(ROWS, width),
            b_in.reshape(ROWS, STATE),
            c_in.reshape(ROWS, STATE),
            jnp.swapaxes(decay_log, 1, 2),
            qkv.reshape(ROWS, 3 * width),
            block_of,
            norm_gain.reshape(1, width),
        )
        return out.reshape(FRAMES, TILE, width)

    spec = P("tm", "space", None)
    return jax.shard_map(
        shards,
        mesh=mesh,
        in_specs=(spec, spec, spec, spec, spec, P("tm", "space"), P()),
        out_specs=spec,
        check_vma=False,
    )
```

```python
import functools
import math

import jax
import jax.numpy as jnp
from jax import lax
from jax.experimental import pallas as pl
from jax.experimental.pallas import tpu as pltpu
from jax.sharding import PartitionSpec as P

MESH = pl.DeviceIdType.MESH
F32 = jnp.float32
BF16 = jnp.bfloat16
HIGHEST = lax.Precision.HIGHEST

FRAMES = 2
TILE = 128
LANES = 128
ROWS = FRAMES * TILE
STATE = 128
UNIT = STATE // 2
CHUNK = 16
PAD = UNIT + 8


def mixer_kernel(
    pairs, row_len, col_len,
    x_hbm, b_hbm, c_hbm, decay_hbm, qkv_ref, label_hbm, gain_hbm, out_hbm,
    x_ref, b_ref, c_ref, decay_ref, gain_ref, load_sem, qkv_in, v_ones, label_rows, label_cols, scores, weights, labels, att, att_out, run_col, run_row, gram, inside, normed,
    state_out, state_in, before, before_decay, total_in, enter_out, entering,
    qkv_send, qkv_recv, label_send, label_recv, state_send, state_recv,
    total_send, total_recv, enter_send, enter_recv, att_send, att_recv, here_sem, column_sem, out_ref, out_sem,
):
    n_space = pairs
    tm = lax.axis_index("tm")
    z = lax.axis_index("space")
    col = lax.div(tm, row_len)
    j = lax.rem(tm, row_len)
    lane = lax.broadcasted_iota(jnp.int32, (1, LANES), 1)
    first_head = lane < LANES // 2

    def space_peer(d):
        return (tm, lax.rem(z + d, n_space))

    def row_peer(d):
        return (col * row_len + lax.rem(j + d, row_len), z)

    def col_peer(d):
        return (lax.rem(col + d, col_len) * row_len + j, z)

    loads = [
        pltpu.make_async_copy(src, dst, load_sem.at[k])
        for k, (src, dst) in enumerate(
            (
                (label_hbm, labels.at[z]),
                (decay_hbm, decay_ref),
                (x_hbm, x_ref),
                (b_hbm, b_ref),
                (c_hbm, c_ref),
                (gain_hbm, gain_ref),
            )
        )
    ]
    for load in loads:
        load.start()

    barrier = pltpu.get_barrier_semaphore()
    leads = z == 0
    for d in range(1, n_space):

        @pl.when(lax.rem(z + d, n_space) != 0)
        def _(d=d):
            pl.semaphore_signal(barrier, inc=1, device_id=space_peer(d), device_id_type=MESH)

    @pl.when(jnp.logical_not(leads))
    def _():
        pl.semaphore_wait(barrier, n_space - 1)
        pl.semaphore_signal(here_sem, inc=1, device_id=(tm, 0), device_id_type=MESH)

    @pl.when(leads)
    def _():
        pl.semaphore_wait(here_sem, n_space - 1)
        for d in range(1, row_len):
            pl.semaphore_signal(barrier, inc=1, device_id=row_peer(d), device_id_type=MESH)
        for d in range(1, col_len):
            pl.semaphore_signal(barrier, inc=1, device_id=col_peer(d), device_id_type=MESH)

    def wait_columns():
        @pl.when(leads)
        def _():
            pl.semaphore_wait(barrier, row_len + col_len - 2)
            for d in range(1, n_space):
                pl.semaphore_signal(
                    column_sem, inc=1, device_id=space_peer(d), device_id_type=MESH
                )

        @pl.when(jnp.logical_not(leads))
        def _():
            pl.semaphore_wait(column_sem, 1)

    def qkv_copy(f, part, d, slot):
        dest = lax.rem(z + d, n_space)
        lanes = pl.ds(pl.multiple_of((part * n_space + dest) * LANES, LANES), LANES)
        return pltpu.make_async_remote_copy(
            src_ref=qkv_ref.at[pl.ds(f * TILE, TILE), lanes],
            dst_ref=qkv_in.at[f, part, slot],
            send_sem=qkv_send.at[f, part, d],
            recv_sem=qkv_recv.at[f, part, d],
            device_id=space_peer(d),
            device_id_type=MESH,
        )

    def qkv_own(f, part):
        lanes = pl.ds(pl.multiple_of((part * n_space + z) * LANES, LANES), LANES)
        return pltpu.make_async_copy(
            qkv_ref.at[pl.ds(f * TILE, TILE), lanes],
            qkv_in.at[f, part, z],
            qkv_recv.at[f, part, 0],
        )

    def label_copy(d, slot):
        return pltpu.make_async_remote_copy(
            src_ref=label_hbm,
            dst_ref=labels.at[slot],
            send_sem=label_send.at[d],
            recv_sem=label_recv.at[d],
            device_id=space_peer(d),
            device_id_type=MESH,
        )

    order = sorted(range(1, n_space), key=lambda d: -min(d, n_space - d))
    for d in order:
        label_copy(d, z).start()

    def send_qkv(f, part):
        for far, near in zip(order, reversed(order)):
            qkv_copy(f, part, jnp.where(lax.rem(tm, 2) == 0, far, near), z).start()
        qkv_own(f, part).start()

    parts = (1, 2, 0)
    for part in parts:
        send_qkv(0, part)
    for load in loads:
        load.wait()

    rows_at = lax.broadcasted_iota(jnp.int32, (ROWS, ROWS), 0)
    cols_at = lax.broadcasted_iota(jnp.int32, (ROWS, ROWS), 1)
    tri = jnp.where(cols_at <= rows_at, 1.0, 0.0).astype(F32)
    decay_t = jnp.concatenate([decay_ref[f] for f in range(FRAMES)], axis=1)
    running_t = lax.dot_general(
        decay_t, tri, (((1,), (1,)), ((), ())), precision=HIGHEST, preferred_element_type=F32
    )
    running = jnp.concatenate(
        [running_t, jnp.zeros((LANES - 2 * pairs, ROWS), F32)], axis=0
    ).T
    for h in range(2 * pairs):
        run_col[h] = jnp.broadcast_to(running[:, h : h + 1], (ROWS, LANES))
        run_row[h] = running_t[h : h + 1, :]
    b_t = b_ref[...].astype(F32).T.astype(BF16)

    low_tile = lax.broadcasted_iota(jnp.int32, (TILE, TILE), 1) <= lax.broadcasted_iota(
        jnp.int32, (TILE, TILE), 0
    )

    def state_pair(g, _):
        lanes = pl.ds(pl.multiple_of(g * LANES, LANES), LANES)
        merged = jnp.where(first_head, run_col[2 * g], run_col[2 * g + 1])
        last = merged[ROWS - 1 : ROWS, :]
        weighted = (x_ref[:, lanes].astype(F32) * jnp.exp(last - merged)).astype(BF16)
        local_state = jnp.dot(b_t, weighted, preferred_element_type=F32)
        block_decay = jnp.broadcast_to(jnp.exp(last), (PAD - UNIT, LANES))
        for k in range(2):
            state_out[2 * g + k, 0:UNIT, :] = local_state[k * UNIT : (k + 1) * UNIT]
            state_out[2 * g + k, UNIT:PAD, :] = block_decay
        return 0

    def scan_pair(g, _):
        lanes = pl.ds(pl.multiple_of(g * LANES, LANES), LANES)
        x_pair = x_ref[:, lanes]
        early, late = slice(0, TILE), slice(TILE, 2 * TILE)
        first, second = [], []
        for k in range(2):
            h = 2 * g + k

            def mix(rows, cols, masked):
                spread = run_col[h, rows, :] - run_row[h, :, cols]
                if masked:
                    spread = jnp.where(low_tile, spread, -jnp.inf)
                return (gram[rows, cols] * jnp.exp(spread)).astype(BF16)

            first.append(mix(early, early, True))
            second.append(
                jnp.concatenate([mix(late, early, False), mix(late, late, True)], axis=1)
            )
        for rows, mixing, values in (
            (early, first, x_pair[early]),
            (late, second, x_pair),
        ):
            both = jnp.dot(
                jnp.concatenate(mixing, axis=0), values, preferred_element_type=F32
            )
            inside[g, rows, :] = jnp.where(first_head, both[early], both[late])
        return 0

    def state_copy(d, slot):
        return pltpu.make_async_remote_copy(
            src_ref=state_out.at[lax.rem(j + d, row_len)],
            dst_ref=state_in.at[slot],
            send_sem=state_send.at[d],
            recv_sem=state_recv.at[d],
            device_id=row_peer(d),
            device_id_type=MESH,
        )

    def total_copy(d, slot):
        return pltpu.make_async_remote_copy(
            src_ref=total_in.at[col],
            dst_ref=total_in.at[slot],
            send_sem=total_send.at[d],
            recv_sem=total_recv.at[d],
            device_id=col_peer(d),
            device_id_type=MESH,
        )

    def enter_copy(d, slot):
        return pltpu.make_async_remote_copy(
            src_ref=enter_out.at[lax.rem(j + d, row_len)],
            dst_ref=entering.at[slot],
            send_sem=enter_send.at[d],
            recv_sem=enter_recv.at[d],
            device_id=row_peer(d),
            device_id_type=MESH,
        )

    lax.fori_loop(0, pairs, state_pair, 0)
    gram[...] = lax.dot_general(
        c_ref[...], b_ref[...], (((1,), (1,)), ((), ())), preferred_element_type=F32
    )
    lax.fori_loop(0, pairs, scan_pair, 0)
    wait_columns()
    for d in range(1, row_len):
        state_copy(d, j).start()
    state_in[j] = state_out[j]
    for part in parts:
        for d in order:
            qkv_copy(0, part, d, z).wait_send()
        send_qkv(1, part)

    def row_prefix():
        for d in range(1, row_len):
            state_copy(d, lax.rem(j - d + row_len, row_len)).wait_recv()

        def step(i, carried):
            state, through = carried
            before[i] = state
            before_decay[i] = through
            here = state_in[i, UNIT:PAD, :]
            return here[0:1] * state + state_in[i, 0:UNIT, :], here * through

        state, through = lax.fori_loop(
            0, row_len, step, (jnp.zeros((UNIT, LANES), F32), jnp.ones((PAD - UNIT, LANES), F32))
        )
        total_in[col, 0:UNIT, :] = state
        total_in[col, UNIT:PAD, :] = through
        for d in range(1, col_len):
            total_copy(d, col).start()

    def col_prefix():
        for d in range(1, col_len):
            total_copy(d, lax.rem(col - d + col_len, col_len)).wait_recv()
        carry = jnp.zeros((UNIT, LANES), F32)
        for i in range(col_len - 1):
            new = total_in[i, UNIT : UNIT + 1, :] * carry + total_in[i, 0:UNIT, :]
            carry = jnp.where(i < col, new, carry)

        def step(i, _):
            enter_out[i] = before[i] + before_decay[i, 0:1, :] * carry
            return 0

        lax.fori_loop(0, row_len, step, 0)
        for d in range(1, row_len):
            enter_copy(d, j).start()
        entering[j] = enter_out[j]

    def finish_scan():
        for d in range(1, row_len):
            enter_copy(d, lax.rem(j - d + row_len, row_len)).wait_recv()
        rows_half = lax.broadcasted_iota(jnp.int32, (LANES, LANES), 0) < LANES // 2
        cols_half = lax.broadcasted_iota(jnp.int32, (LANES, LANES), 1) < LANES // 2
        averager = jnp.where(rows_half == cols_half, 2.0 / LANES, 0.0).astype(F32)

        def norm_pair(g, _):
            state = jnp.concatenate([entering[2 * g], entering[2 * g + 1]], axis=0)
            high = state.astype(BF16)
            low = (state - high.astype(F32)).astype(BF16)
            c_in = c_ref[...]
            carried = jnp.dot(c_in, high, preferred_element_type=F32) + jnp.dot(
                c_in, low, preferred_element_type=F32
            )
            merged = jnp.where(first_head, run_col[2 * g], run_col[2 * g + 1])
            scanned = inside[g] + jnp.exp(merged) * carried
            mean_sq = jnp.dot(
                scanned * scanned, averager, precision=HIGHEST, preferred_element_type=F32
            )
            lanes = pl.ds(pl.multiple_of(g * LANES, LANES), LANES)
            normed[g] = scanned * lax.rsqrt(mean_sq + 1e-05) * gain_ref[:, lanes]
            return 0

        lax.fori_loop(0, pairs, norm_pair, 0)

    def att_copy(f, d, tile, slot):
        return pltpu.make_async_remote_copy(
            src_ref=att_out.at[f, tile],
            dst_ref=att.at[f, slot],
            send_sem=att_send.at[f, d],
            recv_sem=att_recv.at[f, d],
            device_id=space_peer(d),
            device_id_type=MESH,
        )

    def wait_qkv(f, part):
        for d in order:
            qkv_copy(f, part, d, lax.rem(z - d + n_space, n_space)).wait_recv()
        qkv_own(f, part).wait()

    rate = (LANES // 2) ** (-0.5) * math.log2(math.e)
    def attend(f):
        v_ones[:, 0:LANES] = qkv_in[f, 2].reshape(n_space * TILE, LANES)
        for s in range(n_space):
            row = labels[s, f : f + 1, :].astype(F32)
            label_rows[:, s * LANES : (s + 1) * LANES] = jnp.broadcast_to(row, (CHUNK, LANES))
            label_cols[s] = jnp.broadcast_to(row, (TILE, TILE)).T
        keep = [
            jnp.where(first_head, 1.0, 0.0).astype(BF16),
            jnp.where(first_head, 0.0, 1.0).astype(BF16),
        ]

        def step(i, _):
            offsets = (n_space // 2 - i, n_space // 2 + 1 + i)
            tiles = [lax.rem(z + d, n_space) for d in offsets]
            last = i == n_space // 2 - 1

            qkv_copy(f, 0, n_space - offsets[0], tiles[0]).wait_recv()

            @pl.when(jnp.logical_not(last))
            def _():
                qkv_copy(f, 0, n_space - offsets[1], tiles[1]).wait_recv()

            @pl.when(last)
            def _():
                qkv_own(f, 0).wait()

            query = [qkv_in[f, 0, tile] for tile in tiles]
            rows = jnp.concatenate([q * k for q in query for k in keep], axis=0)
            keys = qkv_in[f, 1].reshape(n_space * TILE, LANES)
            scores[...] = lax.dot_general(
                rows, keys, (((1,), (1,)), ((), ())), preferred_element_type=F32
            )
            for k in range(2):
                for c in range(0, TILE, CHUNK):
                    col = label_cols[tiles[k], c : c + CHUNK, :]
                    same = jnp.concatenate([col] * n_space, axis=1) == label_rows[...]
                    for h in range(2):
                        at = slice((2 * k + h) * TILE + c, (2 * k + h) * TILE + c + CHUNK)
                        masked = jnp.where(same, scores[at, :], -jnp.inf)
                        highest = jnp.max(masked, axis=-1, keepdims=True)
                        weights[at, :] = jnp.exp2((masked - highest) * rate).astype(BF16)
            summed = jnp.dot(
                weights[...], v_ones[...], preferred_element_type=F32
            ).reshape(2, 2, TILE, 2 * LANES)
            merged = jnp.where(first_head, summed[:, 0, :, 0:LANES], summed[:, 1, :, 0:LANES])
            total = jnp.where(first_head, summed[:, 0, :, LANES:], summed[:, 1, :, LANES:])
            result = (merged / total).astype(BF16)
            for k in range(2):
                att_out[f, tiles[k]] = result[k]
            att_copy(f, offsets[0], tiles[0], z).start()

            @pl.when(jnp.logical_not(last))
            def _():
                att_copy(f, offsets[1], tiles[1], z).start()

            return 0

        lax.fori_loop(0, n_space // 2, step, 0)
        att[f, z] = att_out[f, z]

    v_ones[:, LANES : 2 * LANES] = jnp.ones((n_space * TILE, LANES), BF16)
    row_prefix()
    for d in order:
        label_copy(d, lax.rem(z - d + n_space, n_space)).wait_recv()
    for f in range(FRAMES):
        wait_qkv(f, 1)
        wait_qkv(f, 2)
        attend(f)
        if f == 0:
            col_prefix()
    finish_scan()

    def out_copy(f):
        rows = pl.ds(f * TILE, TILE)
        return pltpu.make_async_copy(out_ref.at[rows], out_hbm.at[rows], out_sem.at[f])

    for d in order:
        label_copy(d, z).wait_send()
        for part in parts:
            qkv_copy(1, part, d, z).wait_send()
    for d in range(1, row_len):
        state_copy(d, j).wait_send()
        enter_copy(d, j).wait_send()
    for d in range(1, col_len):
        total_copy(d, col).wait_send()

    for f in range(FRAMES):
        for d in range(1, n_space):
            att_copy(f, d, lax.rem(z + d, n_space), lax.rem(z - d + n_space, n_space)).wait_recv()

        def add_pair(g, _):
            lanes = pl.ds(pl.multiple_of(g * LANES, LANES), LANES)
            rows = slice(f * TILE, (f + 1) * TILE)
            out_ref[rows, lanes] = (normed[g, rows, :] + att[f, g].astype(F32)).astype(BF16)
            return 0

        lax.fori_loop(0, pairs, add_pair, 0)
        out_copy(f).start()

    for f in range(FRAMES):
        for d in order:
            att_copy(f, d, lax.rem(z + d, n_space), z).wait_send()
        out_copy(f).wait()


def solution(mesh):
    n_space = mesh.shape["space"]
    row_len = 16
    col_len = mesh.shape["tm"] // row_len

    def shards(x_in, b_in, c_in, decay_log, qkv, block_of, norm_gain):
        width = x_in.shape[2]
        pairs = width // LANES
        dma = pltpu.SemaphoreType.DMA
        out = pl.pallas_call(
            functools.partial(mixer_kernel, pairs, row_len, col_len),
            out_shape=jax.ShapeDtypeStruct((ROWS, width), BF16),
            in_specs=[pl.BlockSpec(memory_space=pltpu.HBM)] * 7,
            out_specs=pl.BlockSpec(memory_space=pltpu.HBM),
            scratch_shapes=[
                pltpu.VMEM((ROWS, width), BF16),
                pltpu.VMEM((ROWS, STATE), BF16),
                pltpu.VMEM((ROWS, STATE), BF16),
                pltpu.VMEM((FRAMES, 2 * pairs, TILE), F32),
                pltpu.VMEM((1, width), F32),
                dma((6,)),
                pltpu.VMEM((FRAMES, 3, n_space, TILE, LANES), BF16),
                pltpu.VMEM((n_space * TILE, 2 * LANES), BF16),
                pltpu.VMEM((CHUNK, n_space * TILE), F32),
                pltpu.VMEM((n_space, TILE, TILE), F32),
                pltpu.VMEM((4 * TILE, n_space * TILE), F32),
                pltpu.VMEM((4 * TILE, n_space * TILE), BF16),
                pltpu.VMEM((n_space, FRAMES, TILE), jnp.int32),
                pltpu.VMEM((FRAMES, n_space, TILE, LANES), BF16),
                pltpu.VMEM((FRAMES, n_space, TILE, LANES), BF16),
                pltpu.VMEM((2 * pairs, ROWS, LANES), F32),
                pltpu.VMEM((2 * pairs, 1, ROWS), F32),
                pltpu.VMEM((ROWS, ROWS), F32),
                pltpu.VMEM((pairs, ROWS, LANES), F32),
                pltpu.VMEM((pairs, ROWS, LANES), F32),
                pltpu.VMEM((row_len, PAD, LANES), F32),
                pltpu.VMEM((row_len, PAD, LANES), F32),
                pltpu.VMEM((row_len, UNIT, LANES), F32),
                pltpu.VMEM((row_len, PAD - UNIT, LANES), F32),
                pltpu.VMEM((col_len, PAD, LANES), F32),
                pltpu.VMEM((row_len, UNIT, LANES), F32),
                pltpu.VMEM((row_len, UNIT, LANES), F32),
                dma((FRAMES, 3, n_space)),
                dma((FRAMES, 3, n_space)),
                dma((n_space,)),
                dma((n_space,)),
                dma((row_len,)),
                dma((row_len,)),
                dma((col_len,)),
                dma((col_len,)),
                dma((row_len,)),
                dma((row_len,)),
                dma((FRAMES, n_space)),
                dma((FRAMES, n_space)),
                pltpu.SemaphoreType.REGULAR,
                pltpu.SemaphoreType.REGULAR,
                pltpu.VMEM((ROWS, width), BF16),
                dma((FRAMES,)),
            ],
            compiler_params=pltpu.CompilerParams(
                collective_id=0, has_side_effects=True, vmem_limit_bytes=64 * 1024 * 1024
            ),
        )(
            x_in.reshape(ROWS, width),
            b_in.reshape(ROWS, STATE),
            c_in.reshape(ROWS, STATE),
            jnp.swapaxes(decay_log, 1, 2),
            qkv.reshape(ROWS, 3 * width),
            block_of,
            norm_gain.reshape(1, width),
        )
        return out.reshape(FRAMES, TILE, width)

    spec = P("tm", "space", None)
    return jax.shard_map(
        shards,
        mesh=mesh,
        in_specs=(spec, spec, spec, spec, spec, P("tm", "space"), P()),
        out_specs=spec,
        check_vma=False,
    )
```
